32 devices in a mesh: group: 2 (over y), ep: 4 (over x, core), tp: 4 (over z).
Axes of the slice: x: 2, y: 2, z: 4, core: 2. Of those that a mesh axis runs over, the one named last changes fastest.
Arguments:
- tokens: bfloat16 [192, 3072], P(('group', 'ep', 'tp')), parts along dimension 0, may hold values from -6 to 6
- experts: int32 [192, 2], P(('group', 'ep', 'tp')), parts along dimension 0, may hold values from 0 to 3, as said below
- replicas: int32 [192, 2], P(('group', 'ep', 'tp')), parts along dimension 0, may hold values from 0 to 2, as said below
- gates: float32 [192, 2], P(('group', 'ep', 'tp')), parts along dimension 0, may hold values from 0.1 to 1
- w_gate: bfloat16 [16, 3072, 4096], P('ep', None, 'tp'), may hold values from -0.109375 to 0.109375
- w_up: bfloat16 [16, 3072, 4096], P('ep', None, 'tp'), may hold values from -0.109375 to 0.109375
- w_down: bfloat16 [16, 4096, 3072], P('ep', 'tp'), may hold values from -0.0625 to 0.0625
Outputs:
- moe_output: bfloat16 [192, 3072], P(('group', 'ep', 'tp')), parts along dimension 0
The draws below stay inside these ranges and needn't reach their ends.
There are 2 independent parts, one for each index of `group`. The reference program is written for one: setup_inputs(seed, part) draws one part's arguments, and reference() takes and returns one part's arrays. A program takes and returns all parts, laid end to end along the dimension named above; an argument that names none is the same for every part. Nothing has to cross between parts.
Inputs may be any that keep to these rules, and one draw needn't show every extreme that they name: The two experts of a row differ. `replicas`: a replica above 0 stands only beside an expert below 2; the picks of the rows of one device name one instance at most 2 times, exactly 2 times for some instance on every device; the picks of the rows of all devices with one index of tp name one instance at most 8 times, exactly 8 times for some instance.
All inputs are finite; a program needn't handle non-finite values.
Results may differ from the reference program's by a relative error of at most 0.018.
Values may be sent and summed in bfloat16 or wider, within the bound.
A program may use at most 128 MiB of HBM per device.

```python
import jax
import jax.numpy as jnp
from jax import lax

D = 3072
EXPERTS = 4
FF = 8192
SPLIT = 2
TOK_DEV = 6
FF_TP = 1024
RECV = 8
INST = 8
PIECES = 16
TOKENS = 96
N_EP = 4
N_TP = 4


def routed_instances(key):
    base_key = jax.random.fold_in(key, 11)
    key_col, key_other, key_rows, key_flip = jax.random.split(base_key, 4)
    pair_count = EXPERTS
    column_type = jax.random.randint(key_col, (N_TP,), 0, pair_count)
    full_type = jnp.broadcast_to(column_type[None, :], (N_EP, N_TP))
    other_type = (full_type + jax.random.randint(key_other, (N_EP, N_TP), 1, pair_count)) % pair_count
    kinds = jnp.arange(pair_count)[None, None, :]
    unused = (kinds != full_type[:, :, None]) & (kinds != other_type[:, :, None])
    low_rest = jnp.min(jnp.where(unused, kinds, 99), axis=2)
    high_rest = jnp.max(jnp.where(unused, kinds, -1), axis=2)
    row_types = jnp.stack([full_type, full_type, other_type, other_type, low_rest, high_rest], axis=-1)
    row_order = jax.vmap(lambda sub_key: jax.random.permutation(sub_key, TOK_DEV))(jax.random.split(key_rows, N_EP * N_TP)).reshape(N_EP, N_TP, TOK_DEV)
    row_types = jnp.take_along_axis(row_types, row_order, axis=2)
    flip_bit = jax.random.randint(key_flip, (N_EP, N_TP, TOK_DEV), 0, 2)
    first_pick = row_types + EXPERTS * flip_bit
    second = row_types + EXPERTS * (1 - flip_bit)
    both_picks = jnp.stack([first_pick, second], axis=-1)
    return both_picks.reshape(TOKENS, 2).astype(jnp.int32)


def draw_experts(key, part):
    picked = routed_instances(key)
    half_count = EXPERTS // 2
    return jnp.where(picked < EXPERTS, picked, (picked - EXPERTS + 1) % half_count).astype(jnp.int32)


def draw_replicas(key, part):
    picked = routed_instances(key)
    half_count = EXPERTS // 2
    return jnp.where(picked < EXPERTS, 0, 1 + (picked - EXPERTS) // half_count).astype(jnp.int32)


def level_of(rng, extent, cuts, least, largest):
    loudness = 1.0
    for position, shards_of in cuts:
        heights = jax.random.uniform(jax.random.fold_in(jax.random.fold_in(rng, 6), position), (shards_of,), jnp.float32, least / len(cuts), largest / len(cuts))
        loudness = loudness * jnp.repeat(jnp.exp(heights), extent[position] // shards_of).reshape((-1,) + (1,) * (len(extent) - 1 - position))
    return loudness


def noise(stream_key, shape, deviation, limit, cuts=(), held_as=jnp.bfloat16):
    result = jax.random.normal(stream_key, shape, jnp.float32) * deviation
    if len(cuts) > 0:
        result = level_of(stream_key, shape, cuts, -0.22, 0.18) * result
    return jnp.clip(result, min=-limit, max=limit).astype(held_as)


def setup_inputs(seed: int = 0, part: int = 0) -> dict:
    key_of = jax.random.split(jax.random.key(seed), 8)
    own_keys = jax.random.split(jax.random.fold_in(key_of[7], part), 8)
    return {
        "tokens": noise(own_keys[0], (TOKENS, D), 1.0, 6.0, ((0, 16),)),
        "experts": draw_experts(jax.random.fold_in(jax.random.fold_in(key_of[7], part), 71), part),
        "replicas": draw_replicas(jax.random.fold_in(jax.random.fold_in(key_of[7], part), 71), part),
        "gates": jnp.clip(0.1 + 0.9 * jax.random.uniform(own_keys[3], (TOKENS, 2), jnp.float32) ** level_of(own_keys[3], (TOKENS, 2), ((0, 16),), -0.2, 0.2), 0.1, 1.0),
        "w_gate": noise(key_of[4], (PIECES, D, FF // SPLIT), D ** -0.5, 0.109375, ((0, 4), (2, 4))),
        "w_up": noise(key_of[5], (PIECES, D, FF // SPLIT), D ** -0.5, 0.109375, ((0, 4), (2, 4))),
        "w_down": noise(key_of[6], (PIECES, FF // SPLIT, D), FF ** -0.5, 0.0625, ((0, 4), (1, 4))),
    }


def reference(tokens, experts, replicas, gates, w_gate, w_up, w_down):
    hot_count = EXPERTS // 2
    instance = jnp.where(replicas == 0, experts, EXPERTS + (replicas - 1) * hot_count + (experts - 1) % hot_count)
    flat_inst = instance.reshape(-1).astype(jnp.int32)
    pick_total = flat_inst.shape[0]
    most_rows = RECV * N_TP

    def per_instance(inst_id):
        matched = flat_inst == inst_id
        pick_index = jnp.nonzero(matched, size=most_rows, fill_value=0)[0].astype(jnp.int32)
        is_valid = jnp.arange(most_rows) < jnp.sum(matched.astype(jnp.int32))
        row_data = tokens[pick_index // 2]
        total = jnp.zeros((most_rows, D), jnp.float32)
        for half in range(SPLIT):
            piece_id = inst_id * SPLIT + half
            gate_act = jnp.dot(row_data, w_gate[piece_id], preferred_element_type=jnp.float32)
            up_act = jnp.dot(row_data, w_up[piece_id], preferred_element_type=jnp.float32)
            hidden = (jax.nn.silu(gate_act) * up_act).astype(jnp.bfloat16)
            blocks = hidden.reshape(most_rows, N_TP, FF_TP).astype(jnp.float32)
            down_blocks = w_down[piece_id].reshape(N_TP, FF_TP, D).astype(jnp.float32)
            partial_value = jnp.einsum("mtf,tfd->tmd", blocks, down_blocks)
            partial_value = lax.optimization_barrier(partial_value.astype(jnp.bfloat16))
            piece_out = jnp.sum(partial_value.astype(jnp.float32), axis=0).astype(jnp.bfloat16)
            total = total + piece_out.astype(jnp.float32)
        return pick_index, total, is_valid

    indices, outputs, valids = lax.map(per_instance, jnp.arange(INST, dtype=jnp.int32))
    contrib = jnp.where(valids.reshape(-1, 1), outputs.reshape(-1, D), jnp.float32(0.0))
    pick_out = jnp.zeros((pick_total, D), jnp.float32).at[indices.reshape(-1)].add(contrib)
    mixed = jnp.sum(pick_out.reshape(TOKENS, 2, D) * gates[:, :, None], axis=1)
    return mixed.astype(jnp.bfloat16)
```

```python
import functools

import jax
import jax.numpy as jnp
from jax import lax
from jax.experimental import pallas as pl
from jax.experimental.pallas import tpu as pltpu
from jax.sharding import PartitionSpec as P

SPLIT = 2
CAP = 2


def pack_rows(arrived, arrived_flags, recv_most):
    src_count, local_piece, col_count, depth = arrived_flags.shape
    marked = jnp.transpose(arrived_flags.astype(jnp.float32), (2, 1, 0, 3)).reshape(
        col_count, local_piece, src_count * depth
    )
    before = jnp.cumsum(marked, axis=2) - marked
    places = jnp.arange(recv_most, dtype=jnp.float32)
    select = (before[:, :, None, :] == places[None, None, :, None]) & (marked[:, :, None, :] > 0.5)
    select = select.astype(jnp.bfloat16).reshape(
        col_count, local_piece, recv_most, src_count, depth
    )
    packed = jnp.einsum(
        "tqrec,eqtcd->trqd", select, arrived, preferred_element_type=jnp.float32
    ).astype(jnp.bfloat16)
    return (packed.reshape(col_count * recv_most, local_piece, arrived.shape[-1]), select)


def on_device(tokens, experts, replicas, gates, w_gate, w_up, w_down):
    ep_count = lax.axis_size("ep")
    local_piece = w_gate.shape[0]
    piece_count = local_piece * ep_count
    inst_count = piece_count // SPLIT
    expert_count = inst_count // 2
    hot_count = expert_count // 2
    recv_most = CAP * ep_count
    rows_dev, features = tokens.shape
    slot_total = inst_count * CAP
    instance = jnp.where(
        replicas == 0,
        experts,
        expert_count + (replicas - 1) * hot_count + (experts - 1) % hot_count,
    )
    pick_ids = instance.reshape(-1)
    matching = pick_ids[:, None] == pick_ids[None, :]
    positions = jnp.arange(pick_ids.shape[0])
    earlier = positions[:, None] > positions[None, :]
    slot_idx = jnp.sum((matching & earlier).astype(jnp.int32), axis=1)
    target = pick_ids * CAP + slot_idx
    onehot = (jnp.arange(slot_total)[:, None] == target[None, :]).astype(jnp.float32)
    slot_rows = onehot.reshape(slot_total, rows_dev, 2).sum(axis=2)
    inst_rows = jnp.dot(
        slot_rows.astype(jnp.bfloat16), tokens, preferred_element_type=jnp.float32
    ).astype(jnp.bfloat16)
    send_rows = jnp.repeat(inst_rows.reshape(inst_count, CAP, features), SPLIT, axis=0).reshape(
        ep_count, local_piece, CAP, features
    )
    inst_flags = jnp.sum(slot_rows, axis=1).astype(jnp.bfloat16).reshape(inst_count, CAP)
    send_flags = jnp.repeat(inst_flags, SPLIT, axis=0).reshape(ep_count, local_piece, CAP)
    arrived, arrived_flags = (
        lax.all_to_all(send_rows, "ep", split_axis=0, concat_axis=0, tiled=True),
        lax.all_to_all(send_flags, "ep", split_axis=0, concat_axis=0, tiled=True),
    )
    packed, select = pack_rows(arrived[:, :, None], arrived_flags[:, :, None], recv_most)
    own_select = select[0]
    piece = lax.all_gather(packed, "tp", axis=0, tiled=True)
    gate_act = jnp.einsum("rqd,qdf->rqf", piece, w_gate, preferred_element_type=jnp.float32)
    up_act = jnp.einsum("rqd,qdf->rqf", piece, w_up, preferred_element_type=jnp.float32)
    hidden = (jax.nn.silu(gate_act) * up_act).astype(jnp.bfloat16)
    piece = hidden
    summed = lax.psum_scatter(
        jnp.einsum("rqf,qfd->rqd", piece, w_down, preferred_element_type=jnp.float32).astype(
            jnp.bfloat16
        ),
        "tp",
        scatter_dimension=0,
        tiled=True,
    )
    returning = jnp.einsum(
        "qrec,rqd->eqcd", own_select, summed, preferred_element_type=jnp.float32
    ).astype(jnp.bfloat16)
    returned = lax.all_to_all(returning, "ep", split_axis=0, concat_axis=0, tiled=True)
    halves = returned.reshape(inst_count, SPLIT, CAP, features).astype(jnp.float32)
    returned_rows = jnp.sum(halves, axis=1).reshape(slot_total, features)
    weighted = (onehot * gates.reshape(-1)[None, :]).reshape(slot_total, rows_dev, 2).sum(axis=2)
    mixed = jnp.dot(weighted.T, returned_rows, precision=lax.Precision.HIGHEST)
    return mixed.astype(jnp.bfloat16)


COLS = 512
SUB = 8
F32 = jnp.float32
BF16 = jnp.bfloat16


def iota(shape, dim):
    return lax.broadcasted_iota(jnp.int32, shape, dim)


def fused_kernel(n_tp, slots, tokens_ref, experts_ref, replicas_ref, gates_ref, wg, wu, wd, out_ref,
                 ring, stage, blocks, x_all, x_sel, hidden, send_a, keep_a, recv_a, send_b, keep_b,
                 recv_b, send_c, recv_c, w_sem, z_sem, x_sem, c_sem, a_sem, b_sem, t_sem):
    rows_dev, features = tokens_ref.shape
    local_piece, _, units = wg.shape
    local_inst = local_piece // SPLIT
    n_ep = 4
    inst_count = local_inst * n_ep
    expert_count = inst_count // 2
    hot_count = expert_count // 2
    per_inst = CAP * n_ep * n_tp
    segs = features // COLS
    halves = units // COLS
    block_rows = stage.shape[0]
    n_dev = n_ep * n_tp
    tok_rows = n_dev * SUB
    steps = local_piece * halves
    gu_chunks = 2 * steps
    per_slot = features // units

    e = lax.axis_index("ep")
    t = lax.axis_index("tp")
    x, core = e // 2, e % 2
    x_peer = (1 - x) * 2 + core
    core_peer = x * 2 + 1 - core

    def gu_copy(step, which):
        src = wg if which == 0 else wu
        piece, part = step // halves, step % halves
        slot = 2 * step + which
        return pltpu.make_async_copy(
            src.at[piece, :, pl.ds(pl.multiple_of(part * COLS, COLS), COLS)],
            ring.at[slot], w_sem.at[slot, 0])

    def down_place(unit):
        chunk, v = unit // per_slot, unit % per_slot
        return (gu_chunks + chunk) % slots, v

    def down_copy(unit):
        slot, v = down_place(unit)
        col, piece = unit // local_piece, unit % local_piece
        return pltpu.make_async_copy(
            wd.at[piece, :, pl.ds(pl.multiple_of(col * COLS, COLS), COLS)],
            ring.at[slot, pl.ds(pl.multiple_of(v * units, units), units), :],
            w_sem.at[slot, v])

    down_units = segs * local_piece
    down_chunks = down_units // per_slot
    early = min(slots - gu_chunks, down_chunks)

    barrier = pltpu.get_barrier_semaphore()
    for r in range(1, n_tp):
        pl.semaphore_signal(barrier, inc=1, device_id={"tp": (t + r) % n_tp},
                            device_id_type=pl.DeviceIdType.MESH)
    for peer in (x_peer, core_peer):
        pl.semaphore_signal(barrier, inc=1, device_id={"ep": peer},
                            device_id_type=pl.DeviceIdType.MESH)

    def start_weights(step, _):
        gu_copy(step, 0).start()
        gu_copy(step, 1).start()
        return 0

    lax.fori_loop(0, FIRST, start_weights, 0)

    lane = iota((rows_dev, 128), 1)
    coef = jnp.zeros((rows_dev, 128), F32)
    for k in range(2):
        ex = experts_ref[:, k:k + 1]
        rep = replicas_ref[:, k:k + 1]
        hot = (ex + (hot_count - 1)) & (hot_count - 1)
        inst = jnp.where(rep == 0, ex, expert_count + (rep - 1) * hot_count + hot)
        coef = coef + jnp.where(lane == inst, gates_ref[:, k:k + 1], 0.0)
    stage[...] = jnp.zeros_like(stage)
    for s in range(segs):
        stage[s * rows_dev:(s + 1) * rows_dev, :] = tokens_ref[:, s * COLS:(s + 1) * COLS].astype(F32)
    rest = coef
    for j in range(3):
        part = rest.astype(BF16).astype(F32)
        stage[segs * rows_dev:(segs + 1) * rows_dev, j * 128:(j + 1) * 128] = part
        rest = rest - part

    def place(xx, cc, tt):
        return (cc * 2 + xx) * n_tp + tt

    blocks[place(x, core, t)] = stage[...].astype(BF16)
    pl.semaphore_wait(barrier, n_tp + 1)

    def to(where, block, sems, i):
        return pltpu.make_async_remote_copy(
            src_ref=blocks.at[block], dst_ref=blocks.at[block],
            send_sem=sems.at[0, i], recv_sem=sems.at[1, i],
            device_id=where, device_id_type=pl.DeviceIdType.MESH)

    own = [place(x, core, (t + n_tp - r) % n_tp) for r in range(n_tp)]
    other = [place(1 - x, core, (t + n_tp - r) % n_tp) for r in range(n_tp)]
    z_copies = [to({"tp": (t + r) % n_tp}, own[0], z_sem, r - 1) for r in range(1, n_tp)]
    x_copies = [to({"ep": x_peer}, own[r], x_sem, r) for r in range(n_tp)]
    c_copies = [to({"ep": core_peer}, (own + other)[r], c_sem, r) for r in range(2 * n_tp)]
    for copy in z_copies:
        copy.start()
    x_copies[0].start()
    c_copies[0].start()
    lax.fori_loop(FIRST, steps, start_weights, 0)
    for chunk in range(early):
        for v in range(per_slot):
            down_copy(chunk * per_slot + v).start()
    for r in range(1, n_tp):
        z_copies[r - 1].wait_recv()
        x_copies[r].start()
        c_copies[r].start()
    for r in range(n_tp):
        x_copies[r].wait_recv()
        c_copies[n_tp + r].start()
    for r in range(2 * n_tp):
        c_copies[r].wait_recv()
    for copy in z_copies + x_copies + c_copies:
        copy.wait_send()

    arrived = blocks[...].reshape(n_dev * block_rows, COLS)
    pos = iota((tok_rows, n_dev * block_rows), 0)
    n = pos & (SUB - 1)
    rel = iota((tok_rows, n_dev * block_rows), 1) - ((pos >> 3) * block_rows + n)
    rel = jnp.where(n < rows_dev, rel, -1)
    for s in range(segs + 1):
        pick = jnp.where(rel == s * rows_dev, 1.0, 0.0).astype(BF16)
        got = jnp.dot(pick, arrived, preferred_element_type=F32)
        if s < segs:
            x_all[:, s * COLS:(s + 1) * COLS] = got.astype(BF16)
        else:
            coef_all = got[:, 0:128] + got[:, 128:256] + got[:, 256:384]
    coef_t = coef_all.T
    tri = jnp.where(iota((tok_rows, tok_rows), 0) < iota((tok_rows, tok_rows), 1), 1.0, 0.0).astype(BF16)
    sels, gate_cols = [], []
    for i in range(local_inst):
        mine = iota((128, tok_rows), 0) == e * local_inst + i
        row = jnp.sum(jnp.where(mine, coef_t, 0.0), axis=0, keepdims=True)
        weight = jnp.broadcast_to(row, (per_inst, tok_rows))
        marked = jnp.where(weight > 0.0, 1.0, 0.0)
        before = jnp.dot(marked.astype(BF16), tri, preferred_element_type=F32)
        sel = jnp.where(before == iota((per_inst, tok_rows), 0).astype(F32), marked, 0.0)
        gate_cols.append(jnp.sum(sel * weight, axis=1, keepdims=True))
        sels.append(sel)
    sel_all = jnp.concatenate(sels, axis=0)
    spread = sel_all.T.astype(BF16)
    sel_bf = sel_all.astype(BF16)
    for s in range(segs):
        x_sel[:, :, s * COLS:(s + 1) * COLS] = jnp.dot(
            sel_bf, x_all[:, s * COLS:(s + 1) * COLS], preferred_element_type=F32
        ).astype(BF16).reshape(local_inst, per_inst, COLS)

    def up_step(step, _):
        piece, part = step // halves, step % halves
        rows = x_sel[piece // SPLIT]
        gu_copy(step, 0).wait()
        g = jnp.dot(rows, ring[2 * step], preferred_element_type=F32)
        gu_copy(step, 1).wait()
        u = jnp.dot(rows, ring[2 * step + 1], preferred_element_type=F32)
        h = g / (1.0 + jnp.exp(-g)) * u
        hidden[piece, :, pl.ds(pl.multiple_of(part * COLS, COLS), COLS)] = h.astype(BF16)
        for j in range(2):
            chunk = early + 2 * step + j

            @pl.when(chunk < down_chunks)
            def _():
                for v in range(per_slot):
                    down_copy(chunk * per_slot + v).start()
        return 0

    lax.fori_loop(0, steps, up_step, 0)

    half = tok_rows // 2
    quarter = tok_rows // 4

    def a_copy(c):
        return pltpu.make_async_remote_copy(
            src_ref=send_a.at[c], dst_ref=recv_a.at[c],
            send_sem=a_sem.at[0, c], recv_sem=a_sem.at[1, c],
            device_id={"ep": core_peer}, device_id_type=pl.DeviceIdType.MESH)

    def b_copy(c):
        return pltpu.make_async_remote_copy(
            src_ref=send_b.at[c], dst_ref=recv_b.at[c],
            send_sem=b_sem.at[0, c], recv_sem=b_sem.at[1, c],
            device_id={"ep": x_peer}, device_id_type=pl.DeviceIdType.MESH)

    def t_copy(c, r):
        peer = (t + r) % n_tp
        return pltpu.make_async_remote_copy(
            src_ref=send_c.at[c, peer], dst_ref=recv_c.at[c, r - 1],
            send_sem=t_sem.at[0, c, r - 1], recv_sem=t_sem.at[1, c, r - 1],
            device_id={"tp": peer}, device_id_type=pl.DeviceIdType.MESH)

    def stage_a(c):
        parts = []
        for i in range(local_inst):
            total = jnp.zeros((per_inst, COLS), F32)
            for h in range(SPLIT):
                piece = i * SPLIT + h
                unit = c * local_piece + piece
                slot, v = down_place(unit)
                down_copy(unit).wait()
                total = total + jnp.dot(
                    hidden[piece], ring[slot, pl.ds(pl.multiple_of(v * units, units), units), :],
                    preferred_element_type=F32)
            parts.append((total * gate_cols[i]).astype(BF16))
        y = jnp.dot(spread, jnp.concatenate(parts, axis=0), preferred_element_type=F32)
        low, high = y[:half], y[half:]
        send_a[c] = jnp.where(core == 0, high, low).astype(BF16)
        keep_a[c] = jnp.where(core == 0, low, high)
        a_copy(c).start()

    def stage_b(c):
        a_copy(c).wait_recv()
        v = keep_a[c] + recv_a[c].astype(F32)
        low, high = v[:quarter], v[quarter:]
        send_b[c] = jnp.where(x == 0, high, low).astype(BF16)
        keep_b[c] = jnp.where(x == 0, low, high)
        b_copy(c).start()

    def stage_c(c):
        b_copy(c).wait_recv()
        v = keep_b[c] + recv_b[c].astype(F32)
        keep_b[c] = v
        for tt in range(n_tp):
            rows = v[tt * SUB:(tt + 1) * SUB]
            send_c[c, tt] = jnp.concatenate(
                [rows[:, :COLS // 2], rows[:, COLS // 2:]], axis=0).astype(BF16)
        for r in range(1, n_tp):
            t_copy(c, r).start()

    def finish(c):
        rows = keep_b[c, pl.ds(pl.multiple_of(t * SUB, SUB), SUB), :]
        for r in range(1, n_tp):
            t_copy(c, r).wait_recv()
            got = recv_c[c, r - 1].astype(F32)
            rows = rows + jnp.concatenate([got[:SUB], got[SUB:]], axis=1)
        out_ref[:, pl.ds(pl.multiple_of(c * COLS, COLS), COLS)] = rows[:rows_dev].astype(BF16)

    def down_step(c, _):
        stage_a(c)
        for lag, fn in ((1, stage_b), (2, stage_c), (3, finish)):
            @pl.when(c >= lag)
            def _():
                fn(c - lag)
        return 0

    lax.fori_loop(0, segs, down_step, 0)
    stage_b(segs - 1)
    stage_c(segs - 2)
    stage_c(segs - 1)
    for c in range(segs - 3, segs):
        finish(c)

    def drain(c, _):
        a_copy(c).wait_send()
        b_copy(c).wait_send()
        for r in range(1, n_tp):
            t_copy(c, r).wait_send()
        return 0

    lax.fori_loop(0, segs, drain, 0)


FIRST = 2


def fused(n_tp, slots, tokens, experts, replicas, gates, w_gate, w_up, w_down):
    rows_dev, features = tokens.shape
    local_piece, _, units = w_gate.shape
    n_ep = 4
    local_inst = local_piece // SPLIT
    per_inst = CAP * n_ep * n_tp
    n_dev = n_ep * n_tp
    segs = features // COLS
    block_rows = -(-(segs + 1) * rows_dev // 16) * 16
    tok_rows = n_dev * SUB
    per_slot = features // units
    vm = pl.BlockSpec(memory_space=pltpu.VMEM)
    hbm = pl.BlockSpec(memory_space=pl.ANY)
    dma = pltpu.SemaphoreType.DMA
    weights = 3 * local_piece * features * units
    return pl.pallas_call(
        functools.partial(fused_kernel, n_tp, slots),
        out_shape=jax.ShapeDtypeStruct((rows_dev, features), BF16),
        in_specs=[vm] * 4 + [hbm] * 3,
        out_specs=vm,
        scratch_shapes=[
            pltpu.VMEM((slots, features, COLS), BF16),
            pltpu.VMEM((block_rows, COLS), F32),
            pltpu.VMEM((n_dev, block_rows, COLS), BF16),
            pltpu.VMEM((tok_rows, features), BF16),
            pltpu.VMEM((local_inst, per_inst, features), BF16),
            pltpu.VMEM((local_piece, per_inst, units), BF16),
            pltpu.VMEM((segs, tok_rows // 2, COLS), BF16),
            pltpu.VMEM((segs, tok_rows // 2, COLS), F32),
            pltpu.VMEM((segs, tok_rows // 2, COLS), BF16),
            pltpu.VMEM((segs, tok_rows // 4, COLS), BF16),
            pltpu.VMEM((segs, tok_rows // 4, COLS), F32),
            pltpu.VMEM((segs, tok_rows // 4, COLS), BF16),
            pltpu.VMEM((segs, n_tp, 2 * SUB, COLS // 2), BF16),
            pltpu.VMEM((segs, n_tp - 1, 2 * SUB, COLS // 2), BF16),
            dma((slots, per_slot)),
            dma((2, n_tp - 1)),
            dma((2, n_tp)),
            dma((2, 2 * n_tp)),
            dma((2, segs)),
            dma((2, segs)),
            dma((2, segs, n_tp - 1)),
        ],
        compiler_params=pltpu.CompilerParams(
            collective_id=0, has_side_effects=True, vmem_limit_bytes=VMEM_LIMIT
        ),
        cost_estimate=pl.CostEstimate(
            flops=2 * weights * per_inst, bytes_accessed=2 * weights, transcendentals=0
        ),
    )(tokens, experts, replicas, gates, w_gate, w_up, w_down)


VMEM_LIMIT = 64 * 1024 * 1024 - 256 * 1024


def slots_for(n_ep, n_tp, tokens, w_gate):
    rows_dev, features = tokens.shape
    local_piece, _, units = w_gate.shape
    if n_ep != 4 or n_tp < 2 or local_piece % SPLIT or rows_dev > SUB:
        return 0
    hot = local_piece * n_ep // SPLIT // 4
    if features % COLS or units % COLS or features % units or hot & (hot - 1) or n_ep * n_tp * SUB != 128:
        return 0
    chunks = 2 * local_piece * (units // COLS)
    down = (features // COLS) * local_piece
    if down % (features // units):
        return 0
    slots = (56 << 20) // (2 * features * COLS)
    slots = min(slots, chunks + down // (features // units))
    if slots < chunks or chunks + down // (features // units) > slots + chunks:
        return 0
    return slots


def layer(n_ep, n_tp, tokens, experts, replicas, gates, w_gate, w_up, w_down):
    slots = slots_for(n_ep, n_tp, tokens, w_gate)
    args = (tokens, experts, replicas, gates, w_gate, w_up, w_down)
    return fused(n_tp, slots, *args) if slots else on_device(*args)


def solution(mesh):
    return jax.shard_map(
        functools.partial(layer, mesh.shape["ep"], mesh.shape["tp"]),
        mesh=mesh,
        in_specs=(
            P(("group", "ep", "tp"), None),
            P(("group", "ep", "tp"), None),
            P(("group", "ep", "tp"), None),
            P(("group", "ep", "tp"), None),
            P("ep", None, "tp"),
            P("ep", None, "tp"),
            P("ep", "tp", None),
        ),
        out_specs=P(("group", "ep", "tp"), None),
        check_vma=False,
    )
```

```python
import functools

import jax
import jax.numpy as jnp
from jax import lax
from jax.experimental import pallas as pl
from jax.experimental.pallas import tpu as pltpu
from jax.sharding import PartitionSpec as P

SPLIT = 2
CAP = 2


def pack_rows(arrived, arrived_flags, recv_most):
    src_count, local_piece, col_count, depth = arrived_flags.shape
    marked = jnp.transpose(arrived_flags.astype(jnp.float32), (2, 1, 0, 3)).reshape(
        col_count, local_piece, src_count * depth
    )
    before = jnp.cumsum(marked, axis=2) - marked
    places = jnp.arange(recv_most, dtype=jnp.float32)
    select = (before[:, :, None, :] == places[None, None, :, None]) & (marked[:, :, None, :] > 0.5)
    select = select.astype(jnp.bfloat16).reshape(
        col_count, local_piece, recv_most, src_count, depth
    )
    packed = jnp.einsum(
        "tqrec,eqtcd->trqd", select, arrived, preferred_element_type=jnp.float32
    ).astype(jnp.bfloat16)
    return (packed.reshape(col_count * recv_most, local_piece, arrived.shape[-1]), select)


def on_device(tokens, experts, replicas, gates, w_gate, w_up, w_down):
    ep_count = lax.axis_size("ep")
    local_piece = w_gate.shape[0]
    piece_count = local_piece * ep_count
    inst_count = piece_count // SPLIT
    expert_count = inst_count // 2
    hot_count = expert_count // 2
    recv_most = CAP * ep_count
    rows_dev, features = tokens.shape
    slot_total = inst_count * CAP
    instance = jnp.where(
        replicas == 0,
        experts,
        expert_count + (replicas - 1) * hot_count + (experts - 1) % hot_count,
    )
    pick_ids = instance.reshape(-1)
    matching = pick_ids[:, None] == pick_ids[None, :]
    positions = jnp.arange(pick_ids.shape[0])
    earlier = positions[:, None] > positions[None, :]
    slot_idx = jnp.sum((matching & earlier).astype(jnp.int32), axis=1)
    target = pick_ids * CAP + slot_idx
    onehot = (jnp.arange(slot_total)[:, None] == target[None, :]).astype(jnp.float32)
    slot_rows = onehot.reshape(slot_total, rows_dev, 2).sum(axis=2)
    inst_rows = jnp.dot(
        slot_rows.astype(jnp.bfloat16), tokens, preferred_element_type=jnp.float32
    ).astype(jnp.bfloat16)
    send_rows = jnp.repeat(inst_rows.reshape(inst_count, CAP, features), SPLIT, axis=0).reshape(
        ep_count, local_piece, CAP, features
    )
    inst_flags = jnp.sum(slot_rows, axis=1).astype(jnp.bfloat16).reshape(inst_count, CAP)
    send_flags = jnp.repeat(inst_flags, SPLIT, axis=0).reshape(ep_count, local_piece, CAP)
    arrived, arrived_flags = (
        lax.all_to_all(send_rows, "ep", split_axis=0, concat_axis=0, tiled=True),
        lax.all_to_all(send_flags, "ep", split_axis=0, concat_axis=0, tiled=True),
    )
    packed, select = pack_rows(arrived[:, :, None], arrived_flags[:, :, None], recv_most)
    own_select = select[0]
    piece = lax.all_gather(packed, "tp", axis=0, tiled=True)
    gate_act = jnp.einsum("rqd,qdf->rqf", piece, w_gate, preferred_element_type=jnp.float32)
    up_act = jnp.einsum("rqd,qdf->rqf", piece, w_up, preferred_element_type=jnp.float32)
    hidden = (jax.nn.silu(gate_act) * up_act).astype(jnp.bfloat16)
    piece = hidden
    summed = lax.psum_scatter(
        jnp.einsum("rqf,qfd->rqd", piece, w_down, preferred_element_type=jnp.float32).astype(
            jnp.bfloat16
        ),
        "tp",
        scatter_dimension=0,
        tiled=True,
    )
    returning = jnp.einsum(
        "qrec,rqd->eqcd", own_select, summed, preferred_element_type=jnp.float32
    ).astype(jnp.bfloat16)
    returned = lax.all_to_all(returning, "ep", split_axis=0, concat_axis=0, tiled=True)
    halves = returned.reshape(inst_count, SPLIT, CAP, features).astype(jnp.float32)
    returned_rows = jnp.sum(halves, axis=1).reshape(slot_total, features)
    weighted = (onehot * gates.reshape(-1)[None, :]).reshape(slot_total, rows_dev, 2).sum(axis=2)
    mixed = jnp.dot(weighted.T, returned_rows, precision=lax.Precision.HIGHEST)
    return mixed.astype(jnp.bfloat16)


COLS = 512
SUB = 8
F32 = jnp.float32
BF16 = jnp.bfloat16


def iota(shape, dim):
    return lax.broadcasted_iota(jnp.int32, shape, dim)


def fused_kernel(n_tp, slots, tokens_ref, experts_ref, replicas_ref, gates_ref, wg, wu, wd, out_ref,
                 ring, stage, blocks, x_all, x_sel, hidden, send_a, keep_a, recv_a, send_b, keep_b,
                 recv_b, send_c, recv_c, w_sem, z_sem, x_sem, c_sem, a_sem, b_sem, t_sem):
    rows_dev, features = tokens_ref.shape
    local_piece, _, units = wg.shape
    local_inst = local_piece // SPLIT
    n_ep = 4
    inst_count = local_inst * n_ep
    expert_count = inst_count // 2
    hot_count = expert_count // 2
    per_inst = CAP * n_ep * n_tp
    segs = features // COLS
    halves = units // COLS
    block_rows = stage.shape[0]
    n_dev = n_ep * n_tp
    tok_rows = n_dev * SUB
    steps = local_piece * halves
    gu_chunks = 2 * steps
    per_slot = features // units

    e = lax.axis_index("ep")
    t = lax.axis_index("tp")
    x, core = e // 2, e % 2
    x_peer = (1 - x) * 2 + core
    core_peer = x * 2 + 1 - core

    def gu_copy(step, which):
        src = wg if which == 0 else wu
        piece, part = step // halves, step % halves
        slot = 2 * step + which
        return pltpu.make_async_copy(
            src.at[piece, :, pl.ds(pl.multiple_of(part * COLS, COLS), COLS)],
            ring.at[slot], w_sem.at[slot, 0])

    def down_place(unit):
        chunk, v = unit // per_slot, unit % per_slot
        return (gu_chunks + chunk) % slots, v

    def down_copy(unit):
        slot, v = down_place(unit)
        col, piece = unit // local_piece, unit % local_piece
        return pltpu.make_async_copy(
            wd.at[piece, :, pl.ds(pl.multiple_of(col * COLS, COLS), COLS)],
            ring.at[slot, pl.ds(pl.multiple_of(v * units, units), units), :],
            w_sem.at[slot, v])

    down_units = segs * local_piece
    down_chunks = down_units // per_slot
    early = min(slots - gu_chunks, down_chunks)

    barrier = pltpu.get_barrier_semaphore()
    for r in range(1, n_tp):
        pl.semaphore_signal(barrier, inc=1, device_id={"tp": (t + r) % n_tp},
                            device_id_type=pl.DeviceIdType.MESH)
    for peer in (x_peer, core_peer):
        pl.semaphore_signal(barrier, inc=1, device_id={"ep": peer},
                            device_id_type=pl.DeviceIdType.MESH)

    def start_weights(step, _):
        gu_copy(step, 0).start()
        gu_copy(step, 1).start()
        return 0

    lax.fori_loop(0, FIRST, start_weights, 0)

    line = iota((128, rows_dev), 0)
    coef = jnp.zeros((128, rows_dev), F32)
    for k in range(2):
        ex = experts_ref[k:k + 1, :]
        rep = replicas_ref[k:k + 1, :]
        hot = (ex + (hot_count - 1)) & (hot_count - 1)
        inst = jnp.where(rep == 0, ex, expert_count + (rep - 1) * hot_count + hot)
        coef = coef + jnp.where(line == inst, gates_ref[k:k + 1, :], 0.0)
    coef = coef.T
    stage[...] = jnp.zeros_like(stage)
    for s in range(segs):
        stage[s * rows_dev:(s + 1) * rows_dev, :] = tokens_ref[:, s * COLS:(s + 1) * COLS].astype(F32)
    rest = coef
    for j in range(3):
        part = rest.astype(BF16).astype(F32)
        stage[segs * rows_dev:(segs + 1) * rows_dev, j * 128:(j + 1) * 128] = part
        rest = rest - part

    def place(xx, cc, tt):
        return (cc * 2 + xx) * n_tp + tt

    blocks[place(x, core, t)] = stage[...].astype(BF16)
    pl.semaphore_wait(barrier, n_tp + 1)

    def to(where, block, sems, i):
        return pltpu.make_async_remote_copy(
            src_ref=blocks.at[block], dst_ref=blocks.at[block],
            send_sem=sems.at[0, i], recv_sem=sems.at[1, i],
            device_id=where, device_id_type=pl.DeviceIdType.MESH)

    own = [place(x, core, (t + n_tp - r) % n_tp) for r in range(n_tp)]
    other = [place(1 - x, core, (t + n_tp - r) % n_tp) for r in range(n_tp)]
    z_copies = [to({"tp": (t + r) % n_tp}, own[0], z_sem, r - 1) for r in range(1, n_tp)]
    x_copies = [to({"ep": x_peer}, own[r], x_sem, r) for r in range(n_tp)]
    c_copies = [to({"ep": core_peer}, (own + other)[r], c_sem, r) for r in range(2 * n_tp)]
    for copy in z_copies:
        copy.start()
    x_copies[0].start()
    c_copies[0].start()
    started = FIRST

    def start_more(upto):
        upto = min(upto, steps)
        for step in range(started, upto):
            start_weights(step, 0)
        return max(started, upto)

    started = start_more(started + 1)
    for r in range(1, n_tp):
        z_copies[r - 1].wait_recv()
        x_copies[r].start()
        c_copies[r].start()
        started = start_more(started + 1)
    for r in range(n_tp):
        x_copies[r].wait_recv()
        c_copies[n_tp + r].start()
        started = start_more(started + 1)
    started = start_more(steps)
    for chunk in range(early):
        for v in range(per_slot):
            down_copy(chunk * per_slot + v).start()
    for r in range(2 * n_tp):
        c_copies[r].wait_recv()
    for copy in z_copies + x_copies + c_copies:
        copy.wait_send()

    arrived = blocks[...].reshape(n_dev * block_rows, COLS)
    pos = iota((tok_rows, n_dev * block_rows), 0)
    n = pos & (SUB - 1)
    rel = iota((tok_rows, n_dev * block_rows), 1) - ((pos >> 3) * block_rows + n)
    rel = jnp.where(n < rows_dev, rel, -1)
    for s in range(segs + 1):
        pick = jnp.where(rel == s * rows_dev, 1.0, 0.0).astype(BF16)
        got = jnp.dot(pick, arrived, preferred_element_type=F32)
        if s < segs:
            x_all[:, s * COLS:(s + 1) * COLS] = got.astype(BF16)
        else:
            coef_all = got[:, 0:128] + got[:, 128:256] + got[:, 256:384]
    coef_t = coef_all.T
    tri = jnp.where(iota((tok_rows, tok_rows), 0) < iota((tok_rows, tok_rows), 1), 1.0, 0.0).astype(BF16)
    sels, gate_cols = [], []
    for i in range(local_inst):
        mine = iota((128, tok_rows), 0) == e * local_inst + i
        row = jnp.sum(jnp.where(mine, coef_t, 0.0), axis=0, keepdims=True)
        weight = jnp.broadcast_to(row, (per_inst, tok_rows))
        marked = jnp.where(weight > 0.0, 1.0, 0.0)
        before = jnp.dot(marked.astype(BF16), tri, preferred_element_type=F32)
        sel = jnp.where(before == iota((per_inst, tok_rows), 0).astype(F32), marked, 0.0)
        gate_cols.append(jnp.sum(sel * weight, axis=1, keepdims=True))
        sels.append(sel)
    sel_all = jnp.concatenate(sels, axis=0)
    spread = sel_all.T.astype(BF16)
    sel_bf = sel_all.astype(BF16)
    for s in range(segs):
        x_sel[:, :, s * COLS:(s + 1) * COLS] = jnp.dot(
            sel_bf, x_all[:, s * COLS:(s + 1) * COLS], preferred_element_type=F32
        ).astype(BF16).reshape(local_inst, per_inst, COLS)

    def up_step(step, _):
        piece, part = step // halves, step % halves
        rows = x_sel[piece // SPLIT]
        gu_copy(step, 0).wait()
        g = jnp.dot(rows, ring[2 * step], preferred_element_type=F32)
        gu_copy(step, 1).wait()
        u = jnp.dot(rows, ring[2 * step + 1], preferred_element_type=F32)
        h = g / (1.0 + jnp.exp(-g)) * u
        hidden[piece, :, pl.ds(pl.multiple_of(part * COLS, COLS), COLS)] = h.astype(BF16)
        for j in range(2):
            chunk = early + 2 * step + j

            @pl.when(chunk < down_chunks)
            def _():
                for v in range(per_slot):
                    down_copy(chunk * per_slot + v).start()
        return 0

    lax.fori_loop(0, steps, up_step, 0)

    half = tok_rows // 2
    quarter = tok_rows // 4

    def a_copy(c):
        return pltpu.make_async_remote_copy(
            src_ref=send_a.at[c], dst_ref=recv_a.at[c],
            send_sem=a_sem.at[0, c], recv_sem=a_sem.at[1, c],
            device_id={"ep": core_peer}, device_id_type=pl.DeviceIdType.MESH)

    def b_copy(c):
        return pltpu.make_async_remote_copy(
            src_ref=send_b.at[c], dst_ref=recv_b.at[c],
            send_sem=b_sem.at[0, c], recv_sem=b_sem.at[1, c],
            device_id={"ep": x_peer}, device_id_type=pl.DeviceIdType.MESH)

    def t_copy(c, r):
        peer = (t + r) % n_tp
        return pltpu.make_async_remote_copy(
            src_ref=send_c.at[c, peer], dst_ref=recv_c.at[c, r - 1],
            send_sem=t_sem.at[0, c, r - 1], recv_sem=t_sem.at[1, c, r - 1],
            device_id={"tp": peer}, device_id_type=pl.DeviceIdType.MESH)

    def stage_a(c):
        parts = []
        for i in range(local_inst):
            total = jnp.zeros((per_inst, COLS), F32)
            for h in range(SPLIT):
                piece = i * SPLIT + h
                unit = c * local_piece + piece
                slot, v = down_place(unit)
                down_copy(unit).wait()
                total = total + jnp.dot(
                    hidden[piece], ring[slot, pl.ds(pl.multiple_of(v * units, units), units), :],
                    preferred_element_type=F32)
            parts.append((total * gate_cols[i]).astype(BF16))
        y = jnp.dot(spread, jnp.concatenate(parts, axis=0), preferred_element_type=F32)
        low, high = y[:half], y[half:]
        send_a[c] = jnp.where(core == 0, high, low).astype(BF16)
        keep_a[c] = jnp.where(core == 0, low, high)
        a_copy(c).start()

    def stage_b(c):
        a_copy(c).wait_recv()
        v = keep_a[c] + recv_a[c].astype(F32)
        low, high = v[:quarter], v[quarter:]
        send_b[c] = jnp.where(x == 0, high, low).astype(BF16)
        keep_b[c] = jnp.where(x == 0, low, high)
        b_copy(c).start()

    def stage_c(c):
        b_copy(c).wait_recv()
        v = keep_b[c] + recv_b[c].astype(F32)
        keep_b[c] = v
        for tt in range(n_tp):
            rows = v[tt * SUB:(tt + 1) * SUB]
            send_c[c, tt] = jnp.concatenate(
                [rows[:, :COLS // 2], rows[:, COLS // 2:]], axis=0).astype(BF16)
        for r in range(1, n_tp):
            t_copy(c, r).start()

    def finish(c):
        rows = keep_b[c, pl.ds(pl.multiple_of(t * SUB, SUB), SUB), :]
        for r in range(1, n_tp):
            t_copy(c, r).wait_recv()
            got = recv_c[c, r - 1].astype(F32)
            rows = rows + jnp.concatenate([got[:SUB], got[SUB:]], axis=1)
        out_ref[:, pl.ds(pl.multiple_of(c * COLS, COLS), COLS)] = rows[:rows_dev].astype(BF16)

    def down_step(c, _):
        stage_a(c)
        for lag, fn in ((1, stage_b), (2, stage_c), (3, finish)):
            @pl.when(c >= lag)
            def _():
                fn(c - lag)
        return 0

    lax.fori_loop(0, segs, down_step, 0)
    stage_b(segs - 1)
    stage_c(segs - 2)
    stage_c(segs - 1)
    for c in range(segs - 3, segs):
        finish(c)

    def drain(c, _):
        a_copy(c).wait_send()
        b_copy(c).wait_send()
        for r in range(1, n_tp):
            t_copy(c, r).wait_send()
        return 0

    lax.fori_loop(0, segs, drain, 0)


FIRST = 1


def fused(n_tp, slots, tokens, experts, replicas, gates, w_gate, w_up, w_down):
    rows_dev, features = tokens.shape
    local_piece, _, units = w_gate.shape
    n_ep = 4
    local_inst = local_piece // SPLIT
    per_inst = CAP * n_ep * n_tp
    n_dev = n_ep * n_tp
    segs = features // COLS
    block_rows = -(-(segs + 1) * rows_dev // 16) * 16
    tok_rows = n_dev * SUB
    per_slot = features // units
    vm = pl.BlockSpec(memory_space=pltpu.VMEM)
    hbm = pl.BlockSpec(memory_space=pl.ANY)
    dma = pltpu.SemaphoreType.DMA
    weights = 3 * local_piece * features * units
    return pl.pallas_call(
        functools.partial(fused_kernel, n_tp, slots),
        out_shape=jax.ShapeDtypeStruct((rows_dev, features), BF16),
        in_specs=[vm] * 4 + [hbm] * 3,
        out_specs=vm,
        scratch_shapes=[
            pltpu.VMEM((slots, features, COLS), BF16),
            pltpu.VMEM((block_rows, COLS), F32),
            pltpu.VMEM((n_dev, block_rows, COLS), BF16),
            pltpu.VMEM((tok_rows, features), BF16),
            pltpu.VMEM((local_inst, per_inst, features), BF16),
            pltpu.VMEM((local_piece, per_inst, units), BF16),
            pltpu.VMEM((segs, tok_rows // 2, COLS), BF16),
            pltpu.VMEM((segs, tok_rows // 2, COLS), F32),
            pltpu.VMEM((segs, tok_rows // 2, COLS), BF16),
            pltpu.VMEM((segs, tok_rows // 4, COLS), BF16),
            pltpu.VMEM((segs, tok_rows // 4, COLS), F32),
            pltpu.VMEM((segs, tok_rows // 4, COLS), BF16),
            pltpu.VMEM((segs, n_tp, 2 * SUB, COLS // 2), BF16),
            pltpu.VMEM((segs, n_tp - 1, 2 * SUB, COLS // 2), BF16),
            dma((slots, per_slot)),
            dma((2, n_tp - 1)),
            dma((2, n_tp)),
            dma((2, 2 * n_tp)),
            dma((2, segs)),
            dma((2, segs)),
            dma((2, segs, n_tp - 1)),
        ],
        compiler_params=pltpu.CompilerParams(
            collective_id=0, has_side_effects=True, vmem_limit_bytes=VMEM_LIMIT
        ),
        cost_estimate=pl.CostEstimate(
            flops=2 * weights * per_inst, bytes_accessed=2 * weights, transcendentals=0
        ),
    )(tokens, experts.T, replicas.T, gates.T, w_gate, w_up, w_down)


VMEM_LIMIT = 64 * 1024 * 1024 - 256 * 1024


def slots_for(n_ep, n_tp, tokens, w_gate):
    rows_dev, features = tokens.shape
    local_piece, _, units = w_gate.shape
    if n_ep != 4 or n_tp < 2 or local_piece % SPLIT or rows_dev > SUB:
        return 0
    hot = local_piece * n_ep // SPLIT // 4
    if features % COLS or units % COLS or features % units or hot & (hot - 1) or n_ep * n_tp * SUB != 128:
        return 0
    chunks = 2 * local_piece * (units // COLS)
    down = (features // COLS) * local_piece
    if down % (features // units):
        return 0
    slots = (56 << 20) // (2 * features * COLS)
    slots = min(slots, chunks + down // (features // units))
    if slots < chunks or chunks + down // (features // units) > slots + chunks:
        return 0
    return slots


def layer(n_ep, n_tp, tokens, experts, replicas, gates, w_gate, w_up, w_down):
    slots = slots_for(n_ep, n_tp, tokens, w_gate)
    args = (tokens, experts, replicas, gates, w_gate, w_up, w_down)
    return fused(n_tp, slots, *args) if slots else on_device(*args)


def solution(mesh):
    return jax.shard_map(
        functools.partial(layer, mesh.shape["ep"], mesh.shape["tp"]),
        mesh=mesh,
        in_specs=(
            P(("group", "ep", "tp"), None),
            P(("group", "ep", "tp"), None),
            P(("group", "ep", "tp"), None),
            P(("group", "ep", "tp"), None),
            P("ep", None, "tp"),
            P("ep", None, "tp"),
            P("ep", "tp", None),
        ),
        out_specs=P(("group", "ep", "tp"), None),
        check_vma=False,
    )
```

```python
import functools

import jax
import jax.numpy as jnp
from jax import lax
from jax.experimental import pallas as pl
from jax.experimental.pallas import tpu as pltpu
from jax.sharding import PartitionSpec as P

SPLIT = 2
CAP = 2


def pack_rows(arrived, arrived_flags, recv_most):
    src_count, local_piece, col_count, depth = arrived_flags.shape
    marked = jnp.transpose(arrived_flags.astype(jnp.float32), (2, 1, 0, 3)).reshape(
        col_count, local_piece, src_count * depth
    )
    before = jnp.cumsum(marked, axis=2) - marked
    places = jnp.arange(recv_most, dtype=jnp.float32)
    select = (before[:, :, None, :] == places[None, None, :, None]) & (marked[:, :, None, :] > 0.5)
    select = select.astype(jnp.bfloat16).reshape(
        col_count, local_piece, recv_most, src_count, depth
    )
    packed = jnp.einsum(
        "tqrec,eqtcd->trqd", select, arrived, preferred_element_type=jnp.float32
    ).astype(jnp.bfloat16)
    return (packed.reshape(col_count * recv_most, local_piece, arrived.shape[-1]), select)


def on_device(tokens, experts, replicas, gates, w_gate, w_up, w_down):
    ep_count = lax.axis_size("ep")
    local_piece = w_gate.shape[0]
    piece_count = local_piece * ep_count
    inst_count = piece_count // SPLIT
    expert_count = inst_count // 2
    hot_count = expert_count // 2
    recv_most = CAP * ep_count
    rows_dev, features = tokens.shape
    slot_total = inst_count * CAP
    instance = jnp.where(
        replicas == 0,
        experts,
        expert_count + (replicas - 1) * hot_count + (experts - 1) % hot_count,
    )
    pick_ids = instance.reshape(-1)
    matching = pick_ids[:, None] == pick_ids[None, :]
    positions = jnp.arange(pick_ids.shape[0])
    earlier = positions[:, None] > positions[None, :]
    slot_idx = jnp.sum((matching & earlier).astype(jnp.int32), axis=1)
    target = pick_ids * CAP + slot_idx
    onehot = (jnp.arange(slot_total)[:, None] == target[None, :]).astype(jnp.float32)
    slot_rows = onehot.reshape(slot_total, rows_dev, 2).sum(axis=2)
    inst_rows = jnp.dot(
        slot_rows.astype(jnp.bfloat16), tokens, preferred_element_type=jnp.float32
    ).astype(jnp.bfloat16)
    send_rows = jnp.repeat(inst_rows.reshape(inst_count, CAP, features), SPLIT, axis=0).reshape(
        ep_count, local_piece, CAP, features
    )
    inst_flags = jnp.sum(slot_rows, axis=1).astype(jnp.bfloat16).reshape(inst_count, CAP)
    send_flags = jnp.repeat(inst_flags, SPLIT, axis=0).reshape(ep_count, local_piece, CAP)
    arrived, arrived_flags = (
        lax.all_to_all(send_rows, "ep", split_axis=0, concat_axis=0, tiled=True),
        lax.all_to_all(send_flags, "ep", split_axis=0, concat_axis=0, tiled=True),
    )
    packed, select = pack_rows(arrived[:, :, None], arrived_flags[:, :, None], recv_most)
    own_select = select[0]
    piece = lax.all_gather(packed, "tp", axis=0, tiled=True)
    gate_act = jnp.einsum("rqd,qdf->rqf", piece, w_gate, preferred_element_type=jnp.float32)
    up_act = jnp.einsum("rqd,qdf->rqf", piece, w_up, preferred_element_type=jnp.float32)
    hidden = (jax.nn.silu(gate_act) * up_act).astype(jnp.bfloat16)
    piece = hidden
    summed = lax.psum_scatter(
        jnp.einsum("rqf,qfd->rqd", piece, w_down, preferred_element_type=jnp.float32).astype(
            jnp.bfloat16
        ),
        "tp",
        scatter_dimension=0,
        tiled=True,
    )
    returning = jnp.einsum(
        "qrec,rqd->eqcd", own_select, summed, preferred_element_type=jnp.float32
    ).astype(jnp.bfloat16)
    returned = lax.all_to_all(returning, "ep", split_axis=0, concat_axis=0, tiled=True)
    halves = returned.reshape(inst_count, SPLIT, CAP, features).astype(jnp.float32)
    returned_rows = jnp.sum(halves, axis=1).reshape(slot_total, features)
    weighted = (onehot * gates.reshape(-1)[None, :]).reshape(slot_total, rows_dev, 2).sum(axis=2)
    mixed = jnp.dot(weighted.T, returned_rows, precision=lax.Precision.HIGHEST)
    return mixed.astype(jnp.bfloat16)


COLS = 512
SUB = 8
F32 = jnp.float32
BF16 = jnp.bfloat16


def iota(shape, dim):
    return lax.broadcasted_iota(jnp.int32, shape, dim)


def fused_kernel(n_tp, slots, tokens_ref, experts_ref, replicas_ref, gates_ref, wg, wu, wd, out_ref,
                 ring, stage, blocks, x_all, x_sel, hidden, send_a, keep_a, recv_a, send_b, keep_b,
                 recv_b, send_c, recv_c, w_sem, z_sem, x_sem, c_sem, a_sem, b_sem, t_sem):
    rows_dev, features = tokens_ref.shape
    local_piece, _, units = wg.shape
    local_inst = local_piece // SPLIT
    n_ep = 4
    inst_count = local_inst * n_ep
    expert_count = inst_count // 2
    hot_count = expert_count // 2
    per_inst = CAP * n_ep * n_tp
    segs = features // COLS
    halves = units // COLS
    block_rows = stage.shape[0]
    n_dev = n_ep * n_tp
    tok_rows = n_dev * SUB
    steps = local_piece * halves
    gu_chunks = 2 * steps
    per_slot = features // units

    e = lax.axis_index("ep")
    t = lax.axis_index("tp")
    x, core = e // 2, e % 2
    x_peer = (1 - x) * 2 + core
    core_peer = x * 2 + 1 - core

    def gu_copy(step, which):
        src = wg if which == 0 else wu
        piece, part = step // halves, step % halves
        slot = 2 * step + which
        return pltpu.make_async_copy(
            src.at[piece, :, pl.ds(pl.multiple_of(part * COLS, COLS), COLS)],
            ring.at[slot], w_sem.at[slot, 0])

    def down_place(unit):
        chunk, v = unit // per_slot, unit % per_slot
        return (gu_chunks + chunk) % slots, v

    def down_copy(unit):
        slot, v = down_place(unit)
        col, piece = unit // local_piece, unit % local_piece
        return pltpu.make_async_copy(
            wd.at[piece, :, pl.ds(pl.multiple_of(col * COLS, COLS), COLS)],
            ring.at[slot, pl.ds(pl.multiple_of(v * units, units), units), :],
            w_sem.at[slot, v])

    down_units = segs * local_piece
    down_chunks = down_units // per_slot
    early = min(slots - gu_chunks, down_chunks)

    barrier = pltpu.get_barrier_semaphore()
    for r in range(1, n_tp):
        pl.semaphore_signal(barrier, inc=1, device_id={"tp": (t + r) % n_tp},
                            device_id_type=pl.DeviceIdType.MESH)
    for peer in (x_peer, core_peer):
        pl.semaphore_signal(barrier, inc=1, device_id={"ep": peer},
                            device_id_type=pl.DeviceIdType.MESH)

    def start_weights(step, _):
        gu_copy(step, 0).start()
        gu_copy(step, 1).start()
        return 0

    lax.fori_loop(0, FIRST, start_weights, 0)

    line = iota((128, rows_dev), 0)
    coef = jnp.zeros((128, rows_dev), F32)
    for k in range(2):
        ex = experts_ref[k:k + 1, :]
        rep = replicas_ref[k:k + 1, :]
        hot = (ex + (hot_count - 1)) & (hot_count - 1)
        inst = jnp.where(rep == 0, ex, expert_count + (rep - 1) * hot_count + hot)
        coef = coef + jnp.where(line == inst, gates_ref[k:k + 1, :], 0.0)
    coef = coef.T
    stage[...] = jnp.zeros_like(stage)
    for s in range(segs):
        stage[s * rows_dev:(s + 1) * rows_dev, :] = tokens_ref[:, s * COLS:(s + 1) * COLS].astype(F32)
    rest = coef
    for j in range(3):
        part = rest.astype(BF16).astype(F32)
        stage[segs * rows_dev:(segs + 1) * rows_dev, j * 128:(j + 1) * 128] = part
        rest = rest - part

    def place(xx, cc, tt):
        return (cc * 2 + xx) * n_tp + tt

    blocks[place(x, core, t)] = stage[...].astype(BF16)
    pl.semaphore_wait(barrier, n_tp + 1)

    def to(where, block, sems, i):
        return pltpu.make_async_remote_copy(
            src_ref=blocks.at[block], dst_ref=blocks.at[block],
            send_sem=sems.at[0, i], recv_sem=sems.at[1, i],
            device_id=where, device_id_type=pl.DeviceIdType.MESH)

    own = [place(x, core, (t + n_tp - r) % n_tp) for r in range(n_tp)]
    other = [place(1 - x, core, (t + n_tp - r) % n_tp) for r in range(n_tp)]
    z_copies = [to({"tp": (t + r) % n_tp}, own[0], z_sem, r - 1) for r in range(1, n_tp)]
    x_copies = [to({"ep": x_peer}, own[r], x_sem, r) for r in range(n_tp)]
    c_copies = [to({"ep": core_peer}, (own + other)[r], c_sem, r) for r in range(2 * n_tp)]
    for copy in z_copies:
        copy.start()
    x_copies[0].start()
    c_copies[0].start()
    started = FIRST

    def start_more(upto):
        upto = min(upto, steps)
        for step in range(started, upto):
            start_weights(step, 0)
        return max(started, upto)

    started = start_more(started + 1)
    for r in range(1, n_tp):
        z_copies[r - 1].wait_recv()
        x_copies[r].start()
        c_copies[r].start()
        started = start_more(started + 1)
    for r in range(n_tp):
        x_copies[r].wait_recv()
        c_copies[n_tp + r].start()
        started = start_more(started + 1)
    started = start_more(steps)
    for chunk in range(early):
        for v in range(per_slot):
            down_copy(chunk * per_slot + v).start()
    for r in range(2 * n_tp):
        c_copies[r].wait_recv()
    for copy in z_copies + x_copies + c_copies:
        copy.wait_send()

    arrived = blocks[...].reshape(n_dev * block_rows, COLS)
    pos = iota((tok_rows, n_dev * block_rows), 0)
    n = pos & (SUB - 1)
    rel = iota((tok_rows, n_dev * block_rows), 1) - ((pos >> 3) * block_rows + n)
    rel = jnp.where(n < rows_dev, rel, -1)
    for s in range(segs + 1):
        pick = jnp.where(rel == s * rows_dev, 1.0, 0.0).astype(BF16)
        got = jnp.dot(pick, arrived, preferred_element_type=F32)
        if s < segs:
            x_all[:, s * COLS:(s + 1) * COLS] = got.astype(BF16)
        else:
            coef_all = got[:, 0:128] + got[:, 128:256] + got[:, 256:384]
    coef_t = coef_all.T
    tri = jnp.where(iota((tok_rows, tok_rows), 0) < iota((tok_rows, tok_rows), 1), 1.0, 0.0).astype(BF16)
    sels, gate_cols = [], []
    for i in range(local_inst):
        mine = iota((128, tok_rows), 0) == e * local_inst + i
        row = jnp.sum(jnp.where(mine, coef_t, 0.0), axis=0, keepdims=True)
        weight = jnp.broadcast_to(row, (per_inst, tok_rows))
        marked = jnp.where(weight > 0.0, 1.0, 0.0)
        before = jnp.dot(marked.astype(BF16), tri, preferred_element_type=F32)
        sel = jnp.where(before == iota((per_inst, tok_rows), 0).astype(F32), marked, 0.0)
        gate_cols.append(jnp.sum(sel * weight, axis=1, keepdims=True))
        sels.append(sel)
    sel_all = jnp.concatenate(sels, axis=0)
    spread = sel_all.T.astype(BF16)
    sel_bf = sel_all.astype(BF16)
    for s in range(segs):
        x_sel[:, :, s * COLS:(s + 1) * COLS] = jnp.dot(
            sel_bf, x_all[:, s * COLS:(s + 1) * COLS], preferred_element_type=F32
        ).astype(BF16).reshape(local_inst, per_inst, COLS)

    def up_step(step, _):
        piece, part = step // halves, step % halves
        rows = x_sel[piece // SPLIT]
        gu_copy(step, 0).wait()
        g = jnp.dot(rows, ring[2 * step], preferred_element_type=F32)
        gu_copy(step, 1).wait()
        u = jnp.dot(rows, ring[2 * step + 1], preferred_element_type=F32)
        h = g / (1.0 + jnp.exp(-g)) * u
        hidden[piece, :, pl.ds(pl.multiple_of(part * COLS, COLS), COLS)] = h.astype(BF16)
        for j in range(2):
            chunk = early + 2 * step + j

            @pl.when(chunk < down_chunks)
            def _():
                for v in range(per_slot):
                    down_copy(chunk * per_slot + v).start()
        return 0

    lax.fori_loop(0, steps, up_step, 0)

    half = tok_rows // 2
    quarter = tok_rows // 4

    def a_copy(c):
        return pltpu.make_async_remote_copy(
            src_ref=send_a.at[c], dst_ref=recv_a.at[c],
            send_sem=a_sem.at[0, c], recv_sem=a_sem.at[1, c],
            device_id={"ep": core_peer}, device_id_type=pl.DeviceIdType.MESH)

    def b_copy(c):
        return pltpu.make_async_remote_copy(
            src_ref=send_b.at[c], dst_ref=recv_b.at[c],
            send_sem=b_sem.at[0, c], recv_sem=b_sem.at[1, c],
            device_id={"ep": x_peer}, device_id_type=pl.DeviceIdType.MESH)

    def t_copy(c, r):
        peer = (t + r) % n_tp
        return pltpu.make_async_remote_copy(
            src_ref=send_c.at[c, peer], dst_ref=recv_c.at[c, r - 1],
            send_sem=t_sem.at[0, c, r - 1], recv_sem=t_sem.at[1, c, r - 1],
            device_id={"tp": peer}, device_id_type=pl.DeviceIdType.MESH)

    def stage_a(c):
        parts = []
        for i in range(local_inst):
            total = jnp.zeros((per_inst, COLS), F32)
            for h in range(SPLIT):
                piece = i * SPLIT + h
                unit = c * local_piece + piece
                slot, v = down_place(unit)
                down_copy(unit).wait()
                total = total + jnp.dot(
                    hidden[piece], ring[slot, pl.ds(pl.multiple_of(v * units, units), units), :],
                    preferred_element_type=F32)
            parts.append((total * gate_cols[i]).astype(BF16))
        y = jnp.dot(spread, jnp.concatenate(parts, axis=0), preferred_element_type=F32)
        low, high = y[:half], y[half:]
        send_a[c] = jnp.where(core == 0, high, low).astype(BF16)
        keep_a[c] = jnp.where(core == 0, low, high)
        a_copy(c).start()

    def stage_b(c):
        a_copy(c).wait_recv()
        v = keep_a[c] + recv_a[c].astype(F32)
        low, high = v[:quarter], v[quarter:]
        send_b[c] = jnp.where(x == 0, high, low).astype(BF16)
        keep_b[c] = jnp.where(x == 0, low, high)
        b_copy(c).start()

    def stage_c(c):
        b_copy(c).wait_recv()
        v = keep_b[c] + recv_b[c].astype(F32)
        keep_b[c] = v
        for tt in range(n_tp):
            rows = v[tt * SUB:(tt + 1) * SUB]
            send_c[c, tt] = jnp.concatenate(
                [rows[:, :COLS // 2], rows[:, COLS // 2:]], axis=0).astype(BF16)
        for r in range(1, n_tp):
            t_copy(c, r).start()

    def finish(c):
        rows = keep_b[c, pl.ds(pl.multiple_of(t * SUB, SUB), SUB), :]
        for r in range(1, n_tp):
            t_copy(c, r).wait_recv()
            got = recv_c[c, r - 1].astype(F32)
            rows = rows + jnp.concatenate([got[:SUB], got[SUB:]], axis=1)
        out_ref[:, pl.ds(pl.multiple_of(c * COLS, COLS), COLS)] = rows[:rows_dev].astype(BF16)

    def down_step(c, _):
        stage_a(c)
        for lag, fn in ((LAG_B, stage_b), (LAG_C, stage_c)):
            @pl.when(c >= lag)
            def _():
                fn(c - lag)
        return 0

    lax.fori_loop(0, segs, down_step, 0)
    for c in range(segs, segs + LAG_C):
        if 0 <= c - LAG_B < segs:
            stage_b(c - LAG_B)
        if 0 <= c - LAG_C < segs:
            stage_c(c - LAG_C)
    for c in range(segs):
        finish(c)

    def drain(c, _):
        a_copy(c).wait_send()
        b_copy(c).wait_send()
        for r in range(1, n_tp):
            t_copy(c, r).wait_send()
        return 0

    lax.fori_loop(0, segs, drain, 0)


FIRST = 1
LAG_B = 3
LAG_C = 5


def fused(n_tp, slots, tokens, experts, replicas, gates, w_gate, w_up, w_down):
    rows_dev, features = tokens.shape
    local_piece, _, units = w_gate.shape
    n_ep = 4
    local_inst = local_piece // SPLIT
    per_inst = CAP * n_ep * n_tp
    n_dev = n_ep * n_tp
    segs = features // COLS
    block_rows = -(-(segs + 1) * rows_dev // 16) * 16
    tok_rows = n_dev * SUB
    per_slot = features // units
    vm = pl.BlockSpec(memory_space=pltpu.VMEM)
    hbm = pl.BlockSpec(memory_space=pl.ANY)
    dma = pltpu.SemaphoreType.DMA
    weights = 3 * local_piece * features * units
    return pl.pallas_call(
        functools.partial(fused_kernel, n_tp, slots),
        out_shape=jax.ShapeDtypeStruct((rows_dev, features), BF16),
        in_specs=[vm] * 4 + [hbm] * 3,
        out_specs=vm,
        scratch_shapes=[
            pltpu.VMEM((slots, features, COLS), BF16),
            pltpu.VMEM((block_rows, COLS), F32),
            pltpu.VMEM((n_dev, block_rows, COLS), BF16),
            pltpu.VMEM((tok_rows, features), BF16),
            pltpu.VMEM((local_inst, per_inst, features), BF16),
            pltpu.VMEM((local_piece, per_inst, units), BF16),
            pltpu.VMEM((segs, tok_rows // 2, COLS), BF16),
            pltpu.VMEM((segs, tok_rows // 2, COLS), F32),
            pltpu.VMEM((segs, tok_rows // 2, COLS), BF16),
            pltpu.VMEM((segs, tok_rows // 4, COLS), BF16),
            pltpu.VMEM((segs, tok_rows // 4, COLS), F32),
            pltpu.VMEM((segs, tok_rows // 4, COLS), BF16),
            pltpu.VMEM((segs, n_tp, 2 * SUB, COLS // 2), BF16),
            pltpu.VMEM((segs, n_tp - 1, 2 * SUB, COLS // 2), BF16),
            dma((slots, per_slot)),
            dma((2, n_tp - 1)),
            dma((2, n_tp)),
            dma((2, 2 * n_tp)),
            dma((2, segs)),
            dma((2, segs)),
            dma((2, segs, n_tp - 1)),
        ],
        compiler_params=pltpu.CompilerParams(
            collective_id=0, has_side_effects=True, vmem_limit_bytes=VMEM_LIMIT
        ),
        cost_estimate=pl.CostEstimate(
            flops=2 * weights * per_inst, bytes_accessed=2 * weights, transcendentals=0
        ),
    )(tokens, experts.T, replicas.T, gates.T, w_gate, w_up, w_down)


VMEM_LIMIT = 64 * 1024 * 1024 - 256 * 1024


def slots_for(n_ep, n_tp, tokens, w_gate):
    rows_dev, features = tokens.shape
    local_piece, _, units = w_gate.shape
    if n_ep != 4 or n_tp < 2 or local_piece % SPLIT or rows_dev > SUB:
        return 0
    hot = local_piece * n_ep // SPLIT // 4
    if features % COLS or units % COLS or features % units or hot & (hot - 1) or n_ep * n_tp * SUB != 128:
        return 0
    chunks = 2 * local_piece * (units // COLS)
    down = (features // COLS) * local_piece
    if down % (features // units):
        return 0
    slots = (56 << 20) // (2 * features * COLS)
    slots = min(slots, chunks + down // (features // units))
    if slots < chunks or chunks + down // (features // units) > slots + chunks:
        return 0
    return slots


def layer(n_ep, n_tp, tokens, experts, replicas, gates, w_gate, w_up, w_down):
    slots = slots_for(n_ep, n_tp, tokens, w_gate)
    args = (tokens, experts, replicas, gates, w_gate, w_up, w_down)
    return fused(n_tp, slots, *args) if slots else on_device(*args)


def solution(mesh):
    return jax.shard_map(
        functools.partial(layer, mesh.shape["ep"], mesh.shape["tp"]),
        mesh=mesh,
        in_specs=(
            P(("group", "ep", "tp"), None),
            P(("group", "ep", "tp"), None),
            P(("group", "ep", "tp"), None),
            P(("group", "ep", "tp"), None),
            P("ep", None, "tp"),
            P("ep", None, "tp"),
            P("ep", "tp", None),
        ),
        out_specs=P(("group", "ep", "tp"), None),
        check_vma=False,
    )
```

```python
import functools

import jax
import jax.numpy as jnp
from jax import lax
from jax.experimental import pallas as pl
from jax.experimental.pallas import tpu as pltpu
from jax.sharding import PartitionSpec as P

SPLIT = 2
CAP = 2


def pack_rows(arrived, arrived_flags, recv_most):
    src_count, local_piece, col_count, depth = arrived_flags.shape
    marked = jnp.transpose(arrived_flags.astype(jnp.float32), (2, 1, 0, 3)).reshape(
        col_count, local_piece, src_count * depth
    )
    before = jnp.cumsum(marked, axis=2) - marked
    places = jnp.arange(recv_most, dtype=jnp.float32)
    select = (before[:, :, None, :] == places[None, None, :, None]) & (marked[:, :, None, :] > 0.5)
    select = select.astype(jnp.bfloat16).reshape(
        col_count, local_piece, recv_most, src_count, depth
    )
    packed = jnp.einsum(
        "tqrec,eqtcd->trqd", select, arrived, preferred_element_type=jnp.float32
    ).astype(jnp.bfloat16)
    return (packed.reshape(col_count * recv_most, local_piece, arrived.shape[-1]), select)


def on_device(tokens, experts, replicas, gates, w_gate, w_up, w_down):
    ep_count = lax.axis_size("ep")
    local_piece = w_gate.shape[0]
    piece_count = local_piece * ep_count
    inst_count = piece_count // SPLIT
    expert_count = inst_count // 2
    hot_count = expert_count // 2
    recv_most = CAP * ep_count
    rows_dev, features = tokens.shape
    slot_total = inst_count * CAP
    instance = jnp.where(
        replicas == 0,
        experts,
        expert_count + (replicas - 1) * hot_count + (experts - 1) % hot_count,
    )
    pick_ids = instance.reshape(-1)
    matching = pick_ids[:, None] == pick_ids[None, :]
    positions = jnp.arange(pick_ids.shape[0])
    earlier = positions[:, None] > positions[None, :]
    slot_idx = jnp.sum((matching & earlier).astype(jnp.int32), axis=1)
    target = pick_ids * CAP + slot_idx
    onehot = (jnp.arange(slot_total)[:, None] == target[None, :]).astype(jnp.float32)
    slot_rows = onehot.reshape(slot_total, rows_dev, 2).sum(axis=2)
    inst_rows = jnp.dot(
        slot_rows.astype(jnp.bfloat16), tokens, preferred_element_type=jnp.float32
    ).astype(jnp.bfloat16)
    send_rows = jnp.repeat(inst_rows.reshape(inst_count, CAP, features), SPLIT, axis=0).reshape(
        ep_count, local_piece, CAP, features
    )
    inst_flags = jnp.sum(slot_rows, axis=1).astype(jnp.bfloat16).reshape(inst_count, CAP)
    send_flags = jnp.repeat(inst_flags, SPLIT, axis=0).reshape(ep_count, local_piece, CAP)
    arrived, arrived_flags = (
        lax.all_to_all(send_rows, "ep", split_axis=0, concat_axis=0, tiled=True),
        lax.all_to_all(send_flags, "ep", split_axis=0, concat_axis=0, tiled=True),
    )
    packed, select = pack_rows(arrived[:, :, None], arrived_flags[:, :, None], recv_most)
    own_select = select[0]
    piece = lax.all_gather(packed, "tp", axis=0, tiled=True)
    gate_act = jnp.einsum("rqd,qdf->rqf", piece, w_gate, preferred_element_type=jnp.float32)
    up_act = jnp.einsum("rqd,qdf->rqf", piece, w_up, preferred_element_type=jnp.float32)
    hidden = (jax.nn.silu(gate_act) * up_act).astype(jnp.bfloat16)
    piece = hidden
    summed = lax.psum_scatter(
        jnp.einsum("rqf,qfd->rqd", piece, w_down, preferred_element_type=jnp.float32).astype(
            jnp.bfloat16
        ),
        "tp",
        scatter_dimension=0,
        tiled=True,
    )
    returning = jnp.einsum(
        "qrec,rqd->eqcd", own_select, summed, preferred_element_type=jnp.float32
    ).astype(jnp.bfloat16)
    returned = lax.all_to_all(returning, "ep", split_axis=0, concat_axis=0, tiled=True)
    halves = returned.reshape(inst_count, SPLIT, CAP, features).astype(jnp.float32)
    returned_rows = jnp.sum(halves, axis=1).reshape(slot_total, features)
    weighted = (onehot * gates.reshape(-1)[None, :]).reshape(slot_total, rows_dev, 2).sum(axis=2)
    mixed = jnp.dot(weighted.T, returned_rows, precision=lax.Precision.HIGHEST)
    return mixed.astype(jnp.bfloat16)


COLS = 512
SUB = 8
F32 = jnp.float32
BF16 = jnp.bfloat16


def iota(shape, dim):
    return lax.broadcasted_iota(jnp.int32, shape, dim)


def fused_kernel(n_tp, slots, tokens_ref, experts_ref, replicas_ref, gates_ref, wg, wu, wd, out_ref,
                 ring, stage, blocks, picks, x_all, x_sel, hidden, send_a, keep_a, recv_a, send_b, keep_b,
                 recv_b, send_c, recv_c, w_sem, z_sem, x_sem, c_sem, a_sem, b_sem, t_sem):
    rows_dev, features = tokens_ref.shape
    local_piece, _, units = wg.shape
    local_inst = local_piece // SPLIT
    n_ep = 4
    inst_count = local_inst * n_ep
    expert_count = inst_count // 2
    hot_count = expert_count // 2
    per_inst = CAP * n_ep * n_tp
    segs = features // COLS
    halves = units // COLS
    block_rows = stage.shape[0]
    n_dev = n_ep * n_tp
    tok_rows = n_dev * SUB
    steps = local_piece * halves
    gu_chunks = 2 * steps
    per_slot = features // units

    e = lax.axis_index("ep")
    t = lax.axis_index("tp")
    x, core = e // 2, e % 2
    x_peer = (1 - x) * 2 + core
    core_peer = x * 2 + 1 - core

    def gu_copy(step, which):
        src = wg if which == 0 else wu
        piece, part = step // halves, step % halves
        slot = 2 * step + which
        return pltpu.make_async_copy(
            src.at[piece, :, pl.ds(pl.multiple_of(part * COLS, COLS), COLS)],
            ring.at[slot], w_sem.at[slot, 0])

    def down_place(unit):
        chunk, v = unit // per_slot, unit % per_slot
        return (gu_chunks + chunk) % slots, v

    def down_copy(unit):
        slot, v = down_place(unit)
        col, piece = unit // local_piece, unit % local_piece
        return pltpu.make_async_copy(
            wd.at[piece, :, pl.ds(pl.multiple_of(col * COLS, COLS), COLS)],
            ring.at[slot, pl.ds(pl.multiple_of(v * units, units), units), :],
            w_sem.at[slot, v])

    down_units = segs * local_piece
    down_chunks = down_units // per_slot
    early = min(slots - gu_chunks, down_chunks)

    barrier = pltpu.get_barrier_semaphore()
    for r in range(1, n_tp):
        pl.semaphore_signal(barrier, inc=1, device_id={"tp": (t + r) % n_tp},
                            device_id_type=pl.DeviceIdType.MESH)
    for peer in (x_peer, core_peer):
        pl.semaphore_signal(barrier, inc=1, device_id={"ep": peer},
                            device_id_type=pl.DeviceIdType.MESH)

    def start_weights(step, _):
        gu_copy(step, 0).start()
        gu_copy(step, 1).start()
        return 0

    lax.fori_loop(0, FIRST, start_weights, 0)

    line = iota((128, rows_dev), 0)
    coef = jnp.zeros((128, rows_dev), F32)
    for k in range(2):
        ex = experts_ref[k:k + 1, :]
        rep = replicas_ref[k:k + 1, :]
        hot = (ex + (hot_count - 1)) & (hot_count - 1)
        inst = jnp.where(rep == 0, ex, expert_count + (rep - 1) * hot_count + hot)
        coef = coef + jnp.where(line == inst, gates_ref[k:k + 1, :], 0.0)
    coef = coef.T
    stage[...] = jnp.zeros_like(stage)
    for s in range(segs):
        stage[s * rows_dev:(s + 1) * rows_dev, :] = tokens_ref[:, s * COLS:(s + 1) * COLS].astype(F32)
    rest = coef
    for j in range(3):
        part = rest.astype(BF16).astype(F32)
        stage[segs * rows_dev:(segs + 1) * rows_dev, j * 128:(j + 1) * 128] = part
        rest = rest - part

    def place(xx, cc, tt):
        return (cc * 2 + xx) * n_tp + tt

    blocks[place(x, core, t)] = stage[...].astype(BF16)
    pl.semaphore_wait(barrier, n_tp + 1)

    def to(where, block, sems, i):
        return pltpu.make_async_remote_copy(
            src_ref=blocks.at[block], dst_ref=blocks.at[block],
            send_sem=sems.at[0, i], recv_sem=sems.at[1, i],
            device_id=where, device_id_type=pl.DeviceIdType.MESH)

    own = [place(x, core, (t + n_tp - r) % n_tp) for r in range(n_tp)]
    other = [place(1 - x, core, (t + n_tp - r) % n_tp) for r in range(n_tp)]
    z_copies = [to({"tp": (t + r) % n_tp}, own[0], z_sem, r - 1) for r in range(1, n_tp)]
    x_copies = [to({"ep": x_peer}, own[r], x_sem, r) for r in range(n_tp)]
    c_copies = [to({"ep": core_peer}, (own + other)[r], c_sem, r) for r in range(2 * n_tp)]
    for copy in z_copies:
        copy.start()
    x_copies[0].start()
    c_copies[0].start()
    started = FIRST

    def start_more(upto):
        upto = min(upto, steps)
        for step in range(started, upto):
            start_weights(step, 0)
        return max(started, upto)

    started = start_more(started + 1)
    pos = iota((tok_rows, n_dev * block_rows), 0)
    n = pos & (SUB - 1)
    rel = iota((tok_rows, n_dev * block_rows), 1) - ((pos >> 3) * block_rows + n)
    rel = jnp.where(n < rows_dev, rel, -1)
    for s in range(segs + 1):
        picks[s] = jnp.where(rel == s * rows_dev, 1.0, 0.0).astype(BF16)
    for r in range(1, n_tp):
        z_copies[r - 1].wait_recv()
        x_copies[r].start()
        c_copies[r].start()
        started = start_more(started + 1)
    for r in range(n_tp):
        x_copies[r].wait_recv()
        c_copies[n_tp + r].start()
        started = start_more(started + 1)
    started = start_more(steps)
    for chunk in range(early):
        for v in range(per_slot):
            down_copy(chunk * per_slot + v).start()
    for r in range(2 * n_tp):
        c_copies[r].wait_recv()
    for copy in z_copies + x_copies + c_copies:
        copy.wait_send()

    arrived = blocks[...].reshape(n_dev * block_rows, COLS)
    for s in range(segs + 1):
        got = jnp.dot(picks[s], arrived, preferred_element_type=F32)
        if s < segs:
            x_all[:, s * COLS:(s + 1) * COLS] = got.astype(BF16)
        else:
            coef_all = got[:, 0:128] + got[:, 128:256] + got[:, 256:384]
    coef_t = coef_all.T
    tri = jnp.where(iota((tok_rows, tok_rows), 0) < iota((tok_rows, tok_rows), 1), 1.0, 0.0).astype(BF16)
    sels, gate_cols = [], []
    for i in range(local_inst):
        mine = iota((128, tok_rows), 0) == e * local_inst + i
        row = jnp.sum(jnp.where(mine, coef_t, 0.0), axis=0, keepdims=True)
        weight = jnp.broadcast_to(row, (per_inst, tok_rows))
        marked = jnp.where(weight > 0.0, 1.0, 0.0)
        before = jnp.dot(marked.astype(BF16), tri, preferred_element_type=F32)
        sel = jnp.where(before == iota((per_inst, tok_rows), 0).astype(F32), marked, 0.0)
        gate_cols.append(jnp.sum(sel * weight, axis=1, keepdims=True))
        sels.append(sel)
    sel_all = jnp.concatenate(sels, axis=0)
    spread = sel_all.T.astype(BF16)
    sel_bf = sel_all.astype(BF16)
    for s in range(segs):
        x_sel[:, :, s * COLS:(s + 1) * COLS] = jnp.dot(
            sel_bf, x_all[:, s * COLS:(s + 1) * COLS], preferred_element_type=F32
        ).astype(BF16).reshape(local_inst, per_inst, COLS)

    def up_step(step, _):
        piece, part = step // halves, step % halves
        rows = x_sel[piece // SPLIT]
        gu_copy(step, 0).wait()
        g = jnp.dot(rows, ring[2 * step], preferred_element_type=F32)
        gu_copy(step, 1).wait()
        u = jnp.dot(rows, ring[2 * step + 1], preferred_element_type=F32)
        h = g / (1.0 + jnp.exp(-g)) * u
        hidden[piece, :, pl.ds(pl.multiple_of(part * COLS, COLS), COLS)] = h.astype(BF16)
        for j in range(2):
            chunk = early + 2 * step + j

            @pl.when(chunk < down_chunks)
            def _():
                for v in range(per_slot):
                    down_copy(chunk * per_slot + v).start()
        return 0

    lax.fori_loop(0, steps, up_step, 0)

    half = tok_rows // 2
    quarter = tok_rows // 4

    def a_copy(c):
        return pltpu.make_async_remote_copy(
            src_ref=send_a.at[c], dst_ref=recv_a.at[c],
            send_sem=a_sem.at[0, c], recv_sem=a_sem.at[1, c],
            device_id={"ep": core_peer}, device_id_type=pl.DeviceIdType.MESH)

    def b_copy(c):
        return pltpu.make_async_remote_copy(
            src_ref=send_b.at[c], dst_ref=recv_b.at[c],
            send_sem=b_sem.at[0, c], recv_sem=b_sem.at[1, c],
            device_id={"ep": x_peer}, device_id_type=pl.DeviceIdType.MESH)

    def t_copy(c, r):
        peer = (t + r) % n_tp
        return pltpu.make_async_remote_copy(
            src_ref=send_c.at[c, peer], dst_ref=recv_c.at[c, r - 1],
            send_sem=t_sem.at[0, c, r - 1], recv_sem=t_sem.at[1, c, r - 1],
            device_id={"tp": peer}, device_id_type=pl.DeviceIdType.MESH)

    def stage_a(c):
        parts = []
        for i in range(local_inst):
            total = jnp.zeros((per_inst, COLS), F32)
            for h in range(SPLIT):
                piece = i * SPLIT + h
                unit = c * local_piece + piece
                slot, v = down_place(unit)
                down_copy(unit).wait()
                total = total + jnp.dot(
                    hidden[piece], ring[slot, pl.ds(pl.multiple_of(v * units, units), units), :],
                    preferred_element_type=F32)
            parts.append((total * gate_cols[i]).astype(BF16))
        y = jnp.dot(spread, jnp.concatenate(parts, axis=0), preferred_element_type=F32)
        low, high = y[:half], y[half:]
        send_a[c] = jnp.where(core == 0, high, low).astype(BF16)
        keep_a[c] = jnp.where(core == 0, low, high)
        a_copy(c).start()

    def stage_b(c):
        a_copy(c).wait_recv()
        v = keep_a[c] + recv_a[c].astype(F32)
        low, high = v[:quarter], v[quarter:]
        send_b[c] = jnp.where(x == 0, high, low).astype(BF16)
        keep_b[c] = jnp.where(x == 0, low, high)
        b_copy(c).start()

    def stage_c(c):
        b_copy(c).wait_recv()
        v = keep_b[c] + recv_b[c].astype(F32)
        keep_b[c] = v
        for tt in range(n_tp):
            rows = v[tt * SUB:(tt + 1) * SUB]
            send_c[c, tt] = jnp.concatenate(
                [rows[:, :COLS // 2], rows[:, COLS // 2:]], axis=0).astype(BF16)
        for r in range(1, n_tp):
            t_copy(c, r).start()

    def finish(c):
        rows = keep_b[c, pl.ds(pl.multiple_of(t * SUB, SUB), SUB), :]
        for r in range(1, n_tp):
            t_copy(c, r).wait_recv()
            got = recv_c[c, r - 1].astype(F32)
            rows = rows + jnp.concatenate([got[:SUB], got[SUB:]], axis=1)
        out_ref[:, pl.ds(pl.multiple_of(c * COLS, COLS), COLS)] = rows[:rows_dev].astype(BF16)

    def down_step(c, _):
        stage_a(c)
        for lag, fn in ((LAG_B, stage_b), (LAG_C, stage_c)):
            @pl.when(c >= lag)
            def _():
                fn(c - lag)
        return 0

    lax.fori_loop(0, segs, down_step, 0)
    for c in range(segs, segs + LAG_C):
        if 0 <= c - LAG_B < segs:
            stage_b(c - LAG_B)
        if 0 <= c - LAG_C < segs:
            stage_c(c - LAG_C)
    for c in range(segs):
        finish(c)

    def drain(c, _):
        a_copy(c).wait_send()
        b_copy(c).wait_send()
        for r in range(1, n_tp):
            t_copy(c, r).wait_send()
        return 0

    lax.fori_loop(0, segs, drain, 0)


FIRST = 1
LAG_B = 3
LAG_C = 5


def fused(n_tp, slots, tokens, experts, replicas, gates, w_gate, w_up, w_down):
    rows_dev, features = tokens.shape
    local_piece, _, units = w_gate.shape
    n_ep = 4
    local_inst = local_piece // SPLIT
    per_inst = CAP * n_ep * n_tp
    n_dev = n_ep * n_tp
    segs = features // COLS
    block_rows = -(-(segs + 1) * rows_dev // 16) * 16
    tok_rows = n_dev * SUB
    per_slot = features // units
    vm = pl.BlockSpec(memory_space=pltpu.VMEM)
    hbm = pl.BlockSpec(memory_space=pl.ANY)
    dma = pltpu.SemaphoreType.DMA
    weights = 3 * local_piece * features * units
    return pl.pallas_call(
        functools.partial(fused_kernel, n_tp, slots),
        out_shape=jax.ShapeDtypeStruct((rows_dev, features), BF16),
        in_specs=[vm] * 4 + [hbm] * 3,
        out_specs=vm,
        scratch_shapes=[
            pltpu.VMEM((slots, features, COLS), BF16),
            pltpu.VMEM((block_rows, COLS), F32),
            pltpu.VMEM((n_dev, block_rows, COLS), BF16),
            pltpu.VMEM((segs + 1, tok_rows, n_dev * block_rows), BF16),
            pltpu.VMEM((tok_rows, features), BF16),
            pltpu.VMEM((local_inst, per_inst, features), BF16),
            pltpu.VMEM((local_piece, per_inst, units), BF16),
            pltpu.VMEM((segs, tok_rows // 2, COLS), BF16),
            pltpu.VMEM((segs, tok_rows // 2, COLS), F32),
            pltpu.VMEM((segs, tok_rows // 2, COLS), BF16),
            pltpu.VMEM((segs, tok_rows // 4, COLS), BF16),
            pltpu.VMEM((segs, tok_rows // 4, COLS), F32),
            pltpu.VMEM((segs, tok_rows // 4, COLS), BF16),
            pltpu.VMEM((segs, n_tp, 2 * SUB, COLS // 2), BF16),
            pltpu.VMEM((segs, n_tp - 1, 2 * SUB, COLS // 2), BF16),
            dma((slots, per_slot)),
            dma((2, n_tp - 1)),
            dma((2, n_tp)),
            dma((2, 2 * n_tp)),
            dma((2, segs)),
            dma((2, segs)),
            dma((2, segs, n_tp - 1)),
        ],
        compiler_params=pltpu.CompilerParams(
            collective_id=0, has_side_effects=True, vmem_limit_bytes=VMEM_LIMIT
        ),
        cost_estimate=pl.CostEstimate(
            flops=2 * weights * per_inst, bytes_accessed=2 * weights, transcendentals=0
        ),
    )(tokens, experts.T, replicas.T, gates.T, w_gate, w_up, w_down)


VMEM_LIMIT = 64 * 1024 * 1024 - 256 * 1024


def slots_for(n_ep, n_tp, tokens, w_gate):
    rows_dev, features = tokens.shape
    local_piece, _, units = w_gate.shape
    if n_ep != 4 or n_tp < 2 or local_piece % SPLIT or rows_dev > SUB:
        return 0
    hot = local_piece * n_ep // SPLIT // 4
    if features % COLS or units % COLS or features % units or hot & (hot - 1) or n_ep * n_tp * SUB != 128:
        return 0
    chunks = 2 * local_piece * (units // COLS)
    down = (features // COLS) * local_piece
    if down % (features // units):
        return 0
    slots = (56 << 20) // (2 * features * COLS)
    slots = min(slots, chunks + down // (features // units))
    if slots < chunks or chunks + down // (features // units) > slots + chunks:
        return 0
    return slots


def layer(n_ep, n_tp, tokens, experts, replicas, gates, w_gate, w_up, w_down):
    slots = slots_for(n_ep, n_tp, tokens, w_gate)
    args = (tokens, experts, replicas, gates, w_gate, w_up, w_down)
    return fused(n_tp, slots, *args) if slots else on_device(*args)


def solution(mesh):
    return jax.shard_map(
        functools.partial(layer, mesh.shape["ep"], mesh.shape["tp"]),
        mesh=mesh,
        in_specs=(
            P(("group", "ep", "tp"), None),
            P(("group", "ep", "tp"), None),
            P(("group", "ep", "tp"), None),
            P(("group", "ep", "tp"), None),
            P("ep", None, "tp"),
            P("ep", None, "tp"),
            P("ep", "tp", None),
        ),
        out_specs=P(("group", "ep", "tp"), None),
        check_vma=False,
    )
```
